128 devices in a mesh: dp: 8 (over y, core), vocab: 16 (over x, z).
Axes of the slice: x: 4, y: 4, z: 4, core: 2. Of those that a mesh axis runs over, the one named last changes fastest.
Arguments:
- student_hidden: bfloat16 [896, 4096], P(('dp', 'vocab')), may hold values from -9 to 9
- teacher_hidden: bfloat16 [896, 8192], P(('dp', 'vocab')), may hold values from -9 to 9
- student_head: bfloat16 [98304, 4096], P(('dp', 'vocab'))
- teacher_head: bfloat16 [98304, 8192], P(('dp', 'vocab'))
- token_weight: int32 [896], P(('dp', 'vocab')), may hold values from 0 to 4
- block_count: int32 [8], replicated, may hold values from 2 to 7, as said below
Outputs:
- kl_mean: float32 [], replicated
- hidden_grad: bfloat16 [896, 4096], P(('dp', 'vocab'))
- head_grad: bfloat16 [98304, 4096], P(('dp', 'vocab'))
The draws below stay inside these ranges and needn't reach their ends.
Inputs may be any that keep to these rules, and one draw needn't show every extreme that they name: `block_count`: the counts sum to 24; one data shard holds 7 blocks.
All inputs are finite; a program needn't handle non-finite values.
Results may differ from the reference program's by a relative error of at most 0.005.
Values may be sent and summed in bfloat16 or wider, within the bound.
No kernel may reach another device: no remote copies, remote signals or barrier semaphores. Data moves between devices by JAX's collectives and lax.ppermute only.
A program may use at most 192 MiB of HBM per device.

```python
import math
import jax
import jax.numpy as jnp
from jax import lax

D_STUDENT = 4096
D_TEACHER = 8192
VOC_DEV = 768
BLOCK = 16
CAP = 7
MEAN_BLOCKS = 3
VOCAB = 98304
ROWS = 896
N_DP = 8
N_VOCAB = 16


logit_scale = 3.2


def head_rows(key, salt, indices, width):
    base_key = jax.random.fold_in(key, salt)

    def draw_row(row_index):
        return jax.random.normal(jax.random.fold_in(base_key, row_index), (width,), jnp.float32)
    values = jnp.clip(jax.vmap(draw_row)(indices), -6.0, 6.0)
    return values * (logit_scale / math.sqrt(width))


def drawn_rows(own_key, width):
    return jnp.clip(jax.random.normal(own_key, (ROWS, width), jnp.float32), -6.0, 6.0)


def draw_student_head(key, part):
    return head_rows(key, 11, jnp.arange(VOCAB), D_STUDENT).astype(jnp.bfloat16)


def draw_teacher_head(key, part):
    return head_rows(key, 12, jnp.arange(VOCAB), D_TEACHER).astype(jnp.bfloat16)


def draw_student_hidden(key, part):
    own_key = jax.random.fold_in(key, 21)
    values = drawn_rows(own_key, D_STUDENT)
    return jnp.clip(values, -9.0, 9.0).astype(jnp.bfloat16)


def draw_teacher_hidden(key, part):
    own_key = jax.random.fold_in(key, 22)
    values = drawn_rows(own_key, D_TEACHER)
    return jnp.clip(values, -9.0, 9.0).astype(jnp.bfloat16)


def draw_block_count(key, part):
    own_key = jax.random.fold_in(key, 5)
    subkeys = jax.random.split(own_key, 2)
    busiest = jax.random.randint(subkeys[0], (), 0, N_DP)
    ranking = jax.random.permutation(subkeys[1], N_DP - 1).astype(jnp.int32)
    removal = (CAP - MEAN_BLOCKS + N_DP - 2 - ranking) // (N_DP - 1)
    others = MEAN_BLOCKS - removal
    positions = jnp.arange(N_DP, dtype=jnp.int32)
    source = positions - (positions > busiest).astype(jnp.int32)
    source = jnp.clip(source, 0, N_DP - 2)
    return jnp.where(positions == busiest, CAP, others[source]).astype(jnp.int32)


def with_ends(values, key, low, high):
    longest = values.shape.index(max(values.shape))
    spots = []
    for shift in (0, 1):
        where = [jax.random.randint(jax.random.fold_in(key, axis), (), 0, length) for axis, length in enumerate(values.shape)]
        where[longest] = (where[longest] + shift) % values.shape[longest]
        spots.append(tuple(where))
    return values.at[spots[0]].set(low).at[spots[1]].set(high)


def setup_inputs(seed: int = 0) -> dict:
    key_list = jax.random.split(jax.random.key(seed), 7)
    student_hidden = draw_student_hidden(jax.random.fold_in(key_list[6], 71), 0)
    teacher_hidden = draw_teacher_hidden(jax.random.fold_in(key_list[6], 71), 0)
    student_head = draw_student_head(jax.random.fold_in(key_list[6], 71), 0)
    teacher_head = draw_teacher_head(jax.random.fold_in(key_list[6], 71), 0)
    token_weight = with_ends(jax.random.randint(key_list[4], (ROWS,), 0, 5), jax.random.fold_in(key_list[4], 1), 0, 4).astype(jnp.int32)
    block_count = draw_block_count(jax.random.fold_in(key_list[6], 71), 0)
    return {"student_hidden": student_hidden, "teacher_hidden": teacher_hidden, "student_head": student_head, "teacher_head": teacher_head, "token_weight": token_weight, "block_count": block_count}


def slab_logits(hidden, head):
    return lax.dot_general(hidden, head, (((1,), (1,)), ((), ())), preferred_element_type=jnp.float32)


def reference(student_hidden, teacher_hidden, student_head, teacher_head, token_weight, block_count):
    shard_rows = CAP * BLOCK
    row_ids = jnp.arange(ROWS, dtype=jnp.int32)
    owner_shard = row_ids // shard_rows
    local_row = row_ids % shard_rows
    live_row = local_row < block_count[owner_shard] * BLOCK
    row_weight = jnp.where(live_row, token_weight, 0).astype(jnp.float32)
    slab = VOC_DEV * N_VOCAB
    student_slabs = student_head.reshape(N_DP, slab, D_STUDENT)
    teacher_slabs = teacher_head.reshape(N_DP, slab, D_TEACHER)

    def stats_step(running, head_pair):
        top_t, sum_t, cross_sum, top_s, sum_s = running
        teacher_logits = slab_logits(teacher_hidden, head_pair[1])
        student_logits = slab_logits(student_hidden, head_pair[0])
        new_t = jnp.maximum(top_t, jnp.max(teacher_logits, axis=1))
        new_s = jnp.maximum(top_s, jnp.max(student_logits, axis=1))
        factor_t = jnp.exp(top_t - new_t)
        factor_s = jnp.exp(top_s - new_s)
        exp_t = jnp.exp(teacher_logits - new_t[:, None])
        exp_s = jnp.exp(student_logits - new_s[:, None])
        sum_t = sum_t * factor_t + jnp.sum(exp_t, axis=1)
        cross_sum = cross_sum * factor_t + jnp.sum(exp_t * (teacher_logits - student_logits), axis=1)
        sum_s = sum_s * factor_s + jnp.sum(exp_s, axis=1)
        return (new_t, sum_t, cross_sum, new_s, sum_s), None

    lowest = jnp.full((ROWS,), -jnp.inf, dtype=jnp.float32)
    nought = jnp.zeros((ROWS,), dtype=jnp.float32)
    running, unused = lax.scan(stats_step, (lowest, nought, nought, lowest, nought), (student_slabs, teacher_slabs))
    top_t, sum_t, cross_sum, top_s, sum_s = running
    log_zt = top_t + jnp.log(sum_t)
    log_zs = top_s + jnp.log(sum_s)
    divergence = cross_sum / sum_t - log_zt + log_zs
    kl_mean = jnp.sum(row_weight * divergence) / (MEAN_BLOCKS * N_DP * BLOCK)

    def grad_step(grad_total, head_pair):
        teacher_logits = slab_logits(teacher_hidden, head_pair[1])
        student_logits = slab_logits(student_hidden, head_pair[0])
        teacher_prob = jnp.exp(teacher_logits - log_zt[:, None])
        student_prob = jnp.exp(student_logits - log_zs[:, None])
        logit_grad = (row_weight[:, None] * (student_prob - teacher_prob)).astype(jnp.bfloat16)
        grad_total = grad_total + jnp.dot(logit_grad, head_pair[0], preferred_element_type=jnp.float32)
        slab_grad = lax.dot_general(logit_grad, student_hidden, (((0,), (0,)), ((), ())), preferred_element_type=jnp.float32)
        return grad_total, slab_grad.astype(jnp.bfloat16)

    grad_total, slab_grads = lax.scan(grad_step, jnp.zeros((ROWS, D_STUDENT), dtype=jnp.float32), (student_slabs, teacher_slabs))
    return kl_mean, grad_total.astype(jnp.bfloat16), slab_grads.reshape(VOCAB, D_STUDENT)
```

```python
import jax
import jax.numpy as jnp
from jax import lax
from jax.experimental import pallas as pl
from jax.experimental.pallas import tpu as pltpu
from jax.sharding import PartitionSpec as P

BLOCK = 16
LIVE = 384
OWN = 7
VOC = 768
DT = 8192
DS = 4096
AXES = ("dp", "vocab")
F32 = jnp.float32
BF16 = jnp.bfloat16
NT = (((1,), (1,)), ((), ()))
NN = (((1,), (0,)), ((), ()))


def flat(y, c, x, z):
    return ((y * 2 + c) * 4 + x) * 4 + z


def perm_of(move):
    return [
        (flat(y, c, x, z), flat(*move(y, c, x, z)))
        for y in range(4)
        for c in range(2)
        for x in range(4)
        for z in range(4)
    ]


def minor(shift):
    return perm_of(
        lambda y, c, x, z: (y, c, (x + shift) % 4, z) if c == 0 else ((y + shift) % 4, c, x, z)
    )


def major(shift):
    return perm_of(
        lambda y, c, x, z: ((y + shift) % 4, c, x, z) if c == 0 else (y, c, (x + shift) % 4, z)
    )


SWAP = perm_of(lambda y, c, x, z: (y, 1 - c, x, z))


def permute(value, pairs):
    return lax.ppermute(value, AXES, pairs)


def unit_table(y, x, core, sign):
    k = jnp.arange(4, dtype=jnp.int32)[:, None]
    l = jnp.arange(4, dtype=jnp.int32)[None, :]
    step_y = jnp.where(core == 0, k, l)
    step_x = jnp.where(core == 0, l, k)
    yy = (y + sign * step_y + 4) % 4
    xx = (x + sign * step_x + 4) % 4
    return (yy * 2 + core) * 4 + xx


def params(limit_mib):
    return pltpu.CompilerParams(
        dimension_semantics=("arbitrary",), vmem_limit_bytes=limit_mib * 1024 * 1024
    )


def logits_call(table, stacks, teacher_head, student_head, prior, last):
    n = len(stacks)
    steps = 4 * n

    def kernel(table_ref, *refs):
        stack_refs = refs[:n]
        ht_ref, hs_ref = refs[n], refs[n + 1]
        pos = n + 2
        if prior is not None:
            pt_ref, ps_ref = refs[pos], refs[pos + 1]
            pos += 2
        t_ref, s_ref = refs[pos], refs[pos + 1]
        pos += 2
        if last:
            stat_ref = refs[pos]
            pos += 1
        rows_ref = refs[pos]
        i = pl.program_id(0)
        for k in range(n):
            @pl.when(i // 4 == k)
            def _(k=k):
                rows_ref[...] = stack_refs[k][0]

        add_t = lax.dot_general(ht_ref[...], rows_ref[:, :256], NT, preferred_element_type=F32)
        add_s = lax.dot_general(hs_ref[...], rows_ref[:, 256:], NT, preferred_element_type=F32)

        @pl.when(i == 0)
        def _():
            if prior is None:
                t_ref[...] = add_t
                s_ref[...] = add_s
            else:
                t_ref[...] = pt_ref[...] + add_t
                s_ref[...] = ps_ref[...] + add_s

        @pl.when(i > 0)
        def _():
            t_ref[...] += add_t
            s_ref[...] += add_s

        if last:
            @pl.when(i == steps - 1)
            def _():
                t = t_ref[...]
                s = s_ref[...]
                top_t = jnp.max(t, axis=0, keepdims=True)
                top_s = jnp.max(s, axis=0, keepdims=True)
                exp_t = jnp.exp(t - top_t)
                sum_t = jnp.sum(exp_t, axis=0, keepdims=True)
                cross = jnp.sum(exp_t * (t - s), axis=0, keepdims=True)
                sum_s = jnp.sum(jnp.exp(s - top_s), axis=0, keepdims=True)
                lse_t = top_t + jnp.log(sum_t)
                lse_s = top_s + jnp.log(sum_s)
                mean = cross / sum_t
                for j in range(3):
                    cols = slice(128 * j, 128 * (j + 1))
                    stat_ref[j : j + 1, :] = lse_t[:, cols]
                    stat_ref[3 + j : 4 + j, :] = lse_s[:, cols]
                    stat_ref[8 + j : 9 + j, :] = mean[:, cols]

    whole = pl.BlockSpec((VOC, LIVE), lambda i, tab: (0, 0))
    in_specs = [
        pl.BlockSpec((1, LIVE, LIVE), lambda i, tab, k=k: (jnp.clip(i - 4 * k, 0, 3), 0, 0))
        for k in range(n)
    ] + [
        pl.BlockSpec((VOC, 256), lambda i, tab: (0, tab[i])),
        pl.BlockSpec((VOC, 128), lambda i, tab: (0, tab[i])),
    ]
    args = [*stacks, teacher_head, student_head]
    if prior is not None:
        in_specs += [whole, whole]
        args += list(prior)
    out_specs = [whole, whole]
    out_shape = [jax.ShapeDtypeStruct((VOC, LIVE), F32)] * 2
    if last:
        out_specs.append(pl.BlockSpec((16, 128), lambda i, tab: (0, 0)))
        out_shape.append(jax.ShapeDtypeStruct((16, 128), F32))
    return pl.pallas_call(
        kernel,
        grid_spec=pltpu.PrefetchScalarGridSpec(
            num_scalar_prefetch=1,
            grid=(steps,),
            in_specs=in_specs,
            out_specs=out_specs,
            scratch_shapes=[pltpu.VMEM((LIVE, LIVE), BF16)],
        ),
        out_shape=out_shape,
        compiler_params=params(40),
        cost_estimate=pl.CostEstimate(
            flops=2 * steps * LIVE * LIVE * VOC,
            bytes_accessed=steps * (LIVE + VOC) * LIVE * 2,
            transcendentals=0,
        ),
    )(table, *args)


def logit_grad_call(table, logits_t, logits_s, stat, all_stats, weight, student_head):
    def kernel(tab, t_ref, s_ref, stat_ref, all_ref, w_ref, h0_ref, h1_ref, out_ref, gt_ref, g_ref, kl_ref):
        i = pl.program_id(0)

        @pl.when(i == 0)
        def _():
            every = all_ref[...]
            top = jnp.max(every, axis=0)
            total = top + jnp.log(jnp.sum(jnp.exp(every - top[None]), axis=0))
            log_zt = jnp.concatenate([total[j : j + 1] for j in range(3)], axis=1)
            log_zs = jnp.concatenate([total[3 + j : 4 + j] for j in range(3)], axis=1)
            own_t = jnp.concatenate([stat_ref[j : j + 1, :] for j in range(3)], axis=1)
            mean = jnp.concatenate([stat_ref[8 + j : 9 + j, :] for j in range(3)], axis=1)
            w = w_ref[...]
            grad = (w * (jnp.exp(s_ref[...] - log_zs) - jnp.exp(t_ref[...] - log_zt))).astype(BF16)
            gt_ref[...] = grad
            g_ref[...] = grad.T
            share = jnp.sum(w * mean * jnp.exp(own_t - log_zt), axis=1, keepdims=True)
            common = jnp.sum(w * (log_zs - log_zt), axis=1, keepdims=True)
            kl_ref[0:1, :] = jnp.broadcast_to(share, (1, 128))
            kl_ref[1:2, :] = jnp.broadcast_to(common, (1, 128))

        pair = jnp.concatenate([h0_ref[...], h1_ref[...]], axis=1)
        part = jnp.dot(g_ref[...], pair, preferred_element_type=F32).astype(BF16)
        out_ref[0] = part[:, :128]
        out_ref[1] = part[:, 128:]

    const = lambda *shape: pl.BlockSpec(shape, lambda i, tab: (0,) * len(shape))
    return pl.pallas_call(
        kernel,
        grid_spec=pltpu.PrefetchScalarGridSpec(
            num_scalar_prefetch=1,
            grid=(8,),
            in_specs=[
                const(VOC, LIVE),
                const(VOC, LIVE),
                const(16, 128),
                const(128, 8, 128),
                const(1, LIVE),
                pl.BlockSpec((VOC, 128), lambda i, tab: (0, tab[2 * i])),
                pl.BlockSpec((VOC, 128), lambda i, tab: (0, tab[2 * i + 1])),
            ],
            out_specs=[
                pl.BlockSpec((2, LIVE, 128), lambda i, tab: (i, 0, 0)),
                const(VOC, LIVE),
                const(LIVE, VOC),
                const(8, 128),
            ],
        ),
        out_shape=[
            jax.ShapeDtypeStruct((16, LIVE, 128), BF16),
            jax.ShapeDtypeStruct((VOC, LIVE), BF16),
            jax.ShapeDtypeStruct((LIVE, VOC), BF16),
            jax.ShapeDtypeStruct((8, 128), F32),
        ],
        compiler_params=params(32),
        cost_estimate=pl.CostEstimate(
            flops=2 * LIVE * VOC * 2048, bytes_accessed=8 * 1024 * 1024, transcendentals=VOC * LIVE * 2
        ),
    )(table, logits_t, logits_s, stat, all_stats, weight, student_head, student_head)


def hidden_half_call(table, grad, student_head):
    def kernel(tab, g_ref, h0_ref, h1_ref, out_ref):
        pair = jnp.concatenate([h0_ref[...], h1_ref[...]], axis=1)
        part = jnp.dot(g_ref[...], pair, preferred_element_type=F32)
        out_ref[0] = part[:, :128]
        out_ref[1] = part[:, 128:]

    return pl.pallas_call(
        kernel,
        grid_spec=pltpu.PrefetchScalarGridSpec(
            num_scalar_prefetch=1,
            grid=(8,),
            in_specs=[
                pl.BlockSpec((LIVE, VOC), lambda i, tab: (0, 0)),
                pl.BlockSpec((VOC, 128), lambda i, tab: (0, tab[2 * i])),
                pl.BlockSpec((VOC, 128), lambda i, tab: (0, tab[2 * i + 1])),
            ],
            out_specs=pl.BlockSpec((2, LIVE, 128), lambda i, tab: (i, 0, 0)),
        ),
        out_shape=jax.ShapeDtypeStruct((16, LIVE, 128), F32),
        compiler_params=params(32),
        cost_estimate=pl.CostEstimate(
            flops=2 * LIVE * VOC * 2048, bytes_accessed=7 * 1024 * 1024, transcendentals=0
        ),
    )(table, grad, student_head, student_head)


def head_grad_call(table, stacks, grad_t):
    n = len(stacks)

    def kernel(tab, *refs):
        g_ref, out_ref, rows_ref = refs[n], refs[n + 1], refs[n + 2]
        i = pl.program_id(0)
        for k in range(n):
            @pl.when(i // 4 == k)
            def _(k=k):
                rows_ref[...] = refs[k][0]

        out_ref[...] = jnp.dot(g_ref[...], rows_ref[...], preferred_element_type=F32).astype(BF16)

    return pl.pallas_call(
        kernel,
        grid_spec=pltpu.PrefetchScalarGridSpec(
            num_scalar_prefetch=1,
            grid=(4 * n,),
            in_specs=[
                pl.BlockSpec((1, LIVE, 128), lambda i, tab, k=k: (jnp.clip(i - 4 * k, 0, 3), 0, 2))
                for k in range(n)
            ]
            + [pl.BlockSpec((VOC, LIVE), lambda i, tab: (0, 0))],
            out_specs=pl.BlockSpec((VOC, 128), lambda i, tab: (0, tab[i])),
            scratch_shapes=[pltpu.VMEM((LIVE, 128), BF16)],
        ),
        out_shape=jax.ShapeDtypeStruct((VOC, DS), BF16),
        compiler_params=params(32),
        cost_estimate=pl.CostEstimate(
            flops=4 * LIVE * VOC * DS, bytes_accessed=10 * 1024 * 1024, transcendentals=0
        ),
    )(table, *stacks, grad_t)


def local(student_hidden, teacher_hidden, student_head, teacher_head, token_weight, block_count):
    me = lax.axis_index("dp") * 16 + lax.axis_index("vocab")
    y, core, x = me // 32, (me // 16) % 2, (me // 4) % 4

    units = jnp.concatenate(
        [teacher_hidden.reshape(OWN, 32, 256), student_hidden.reshape(OWN, 32, 128)], axis=2
    ).transpose(1, 0, 2)
    weights = jnp.pad(token_weight.astype(BF16), (0, LIVE - OWN))
    units = jnp.concatenate([units, jnp.broadcast_to(weights, (32, 1, LIVE))], axis=1)
    units = jnp.broadcast_to(units[:, None], (32, 4, 8, LIVE)).reshape(128, 8, LIVE)
    arrived = lax.all_to_all(units, AXES, split_axis=0, concat_axis=0, tiled=True)

    ends = jnp.cumsum(block_count)
    block = jnp.arange(LIVE, dtype=jnp.int32) // BLOCK
    shard = jnp.sum((block[:, None] >= ends[None, :]).astype(jnp.int32), axis=1)
    begin = jnp.sum(jnp.where(jnp.arange(8)[None, :] < shard[:, None], block_count[None, :], 0), axis=1)
    place = (block - begin) * BLOCK + jnp.arange(LIVE, dtype=jnp.int32) % BLOCK
    slot = (shard * 16 + place // OWN) * 8 + place % OWN
    slots = jnp.arange(1024, dtype=jnp.int32)
    pick = (slot[:, None] == slots[None, :]).astype(BF16)
    own = jnp.dot(pick, arrived.reshape(1024, LIVE), preferred_element_type=F32).astype(BF16)
    weight = lax.dot_general(arrived[:, 7, :8].reshape(1, 1024), pick, NT, preferred_element_type=F32)

    stack = jnp.stack([own] + [permute(own, minor(l)) for l in (1, 2, 3)])
    stacks = [stack] + [permute(stack, major(k)) for k in (1, 2, 3)]
    others = [permute(s, SWAP) for s in stacks]
    tab_own = unit_table(y, x, core, -1)
    tab_sib = unit_table(y, x, 1 - core, -1)

    def logits(ks, prior, last):
        table = jnp.concatenate([t[k] for k in ks for t in (tab_own, tab_sib)])
        held = [s[k] for k in ks for s in (stacks, others)]
        return logits_call(table, held, teacher_head, student_head, prior, last)

    logits_t, logits_s = logits((0,), None, False)
    logits_t, logits_s, stat = logits((1, 3, 2), (logits_t, logits_s), True)

    sent = jnp.broadcast_to(stat[None, :8], (128, 8, 128))
    all_stats = lax.all_to_all(sent, AXES, split_axis=0, concat_axis=0, tiled=True)

    dest_own = unit_table(y, x, core, 1).reshape(16)
    dest_sib = unit_table(y, x, 1 - core, 1).reshape(16)
    half, grad_t, grad, kl = logit_grad_call(
        dest_sib, logits_t, logits_s, stat, all_stats, weight, student_head
    )
    half = permute(half, SWAP)
    mine = hidden_half_call(dest_own, grad, student_head)
    head_grad = head_grad_call(
        jnp.concatenate([tab_own.reshape(16), tab_sib.reshape(16)]), [*stacks, *others], grad_t
    )

    total = (mine + half.astype(F32)).reshape(4, 4, LIVE, 128)
    out = total.astype(BF16)
    total = total[0] + sum(permute(out[k], major(k)).astype(F32) for k in (1, 2, 3))
    total = total[0] + sum(permute(total[l], minor(l)) for l in (1, 2, 3))

    share = kl[0, 0]
    hi = share.astype(BF16)
    mid = (share - hi.astype(F32)).astype(BF16)
    low = (share - hi.astype(F32) - mid.astype(F32)).astype(BF16)
    lane = jnp.arange(128)
    extra = jnp.where(lane == 0, hi, jnp.where(lane == 1, mid, jnp.where(lane == 2, low, jnp.zeros((), BF16))))
    back = lax.dot_general(
        pick, total.astype(BF16), (((0,), (0,)), ((), ())), preferred_element_type=F32
    ).astype(BF16)
    back = jnp.where((slots % 8 == 7)[:, None], extra[None, :], back).reshape(128, 8, 128)
    back = lax.all_to_all(back, AXES, split_axis=0, concat_axis=0, tiled=True).astype(F32)
    hidden_grad = jnp.sum(back.reshape(32, 4, 8, 128), axis=1)
    hidden_grad = hidden_grad.transpose(1, 0, 2).reshape(8, DS)[:OWN].astype(BF16)
    kl_mean = (jnp.sum(back[:, 7, :3]) + kl[1, 0]) / LIVE
    return kl_mean, hidden_grad, head_grad


def solution(mesh):
    rows = P(AXES, None)
    return jax.shard_map(
        local,
        mesh=mesh,
        in_specs=(rows, rows, rows, rows, P(AXES), P()),
        out_specs=(P(), rows, rows),
        check_vma=False,
    )
```

```python
import jax
import jax.numpy as jnp
from jax import lax
from jax.experimental import pallas as pl
from jax.experimental.pallas import tpu as pltpu
from jax.sharding import PartitionSpec as P

BLOCK = 16
LIVE = 384
OWN = 7
VOC = 768
DT = 8192
DS = 4096
AXES = ("dp", "vocab")
F32 = jnp.float32
BF16 = jnp.bfloat16
NT = (((1,), (1,)), ((), ()))
TN = (((0,), (0,)), ((), ()))


def flat(y, c, x, z):
    return ((y * 2 + c) * 4 + x) * 4 + z


def perm_of(move):
    return [
        (flat(y, c, x, z), flat(*move(y, c, x, z)))
        for y in range(4)
        for c in range(2)
        for x in range(4)
        for z in range(4)
    ]


def minor(shift):
    return perm_of(
        lambda y, c, x, z: (y, c, (x + shift) % 4, z) if c == 0 else ((y + shift) % 4, c, x, z)
    )


def major(shift):
    return perm_of(
        lambda y, c, x, z: ((y + shift) % 4, c, x, z) if c == 0 else (y, c, (x + shift) % 4, z)
    )


def along_z(shift):
    return perm_of(lambda y, c, x, z: (y, c, x, (z + shift) % 4))


def across():
    return perm_of(
        lambda y, c, x, z: ((y + 2) % 4, c, (x - z) % 4, z) if c == 0 else ((y - z) % 4, c, (x + 2) % 4, z)
    )


SWAP = perm_of(lambda y, c, x, z: (y, 1 - c, x, z))


def permute(value, pairs):
    return lax.ppermute(value, AXES, pairs)


def unit_of(y, c, x):
    return y * 4 + x if c == 0 else 16 + x * 4 + y


BIG = 56
SMEM = pl.BlockSpec(memory_space=pltpu.SMEM)
VMEM = pl.BlockSpec(memory_space=pltpu.VMEM)
HBM = pl.BlockSpec(memory_space=pltpu.HBM)
ANY = pl.BlockSpec(memory_space=pl.ANY)


def params(limit_mib):
    return pltpu.CompilerParams(vmem_limit_bytes=limit_mib * 1024 * 1024)


def cost(flops, nbytes, transcendentals=0):
    return pl.CostEstimate(flops=flops, bytes_accessed=nbytes, transcendentals=transcendentals)


def spread_call(teacher_hidden, student_hidden, token_weight):
    def kernel(t_ref, s_ref, w_ref, out_ref):
        w = jnp.pad(w_ref[...].astype(F32), ((0, 0), (0, 256 - OWN)))
        none = jnp.zeros((1, 128), F32)
        for y in range(4):
            for c in range(2):
                for x in range(4):
                    u = unit_of(y, c, x)
                    t = t_ref[:, 256 * u : 256 * (u + 1)].astype(F32)
                    s = s_ref[:, 128 * u : 128 * (u + 1)].astype(F32)
                    t = jnp.concatenate([t, w], axis=0).astype(BF16)
                    s = jnp.concatenate([s, none], axis=0).astype(BF16)
                    for z in range(4):
                        out_ref[flat(y, c, x, z), :, :256] = t
                        out_ref[flat(y, c, x, z), :, 256:] = s

    return pl.pallas_call(
        kernel,
        grid=(1,),
        in_specs=[
            pl.BlockSpec((OWN, DT), lambda i: (0, 0)),
            pl.BlockSpec((OWN, DS), lambda i: (0, 0)),
            pl.BlockSpec((1, OWN), lambda i: (0, 0)),
        ],
        out_specs=pl.BlockSpec((128, 8, LIVE), lambda i: (0, 0, 0)),
        out_shape=jax.ShapeDtypeStruct((128, 8, LIVE), BF16),
        compiler_params=params(BIG),
        cost_estimate=cost(0, 1 << 20),
    )(teacher_hidden, student_hidden, token_weight.reshape(1, OWN))


def assemble_call(places, parts, after):
    def kernel(at_ref, *refs):
        out_ref = refs[-1]
        for k in range(4):
            out_ref[pl.ds(pl.multiple_of(256 * at_ref[k], 256), 256), :] = refs[k][:256, :]
            out_ref[pl.ds(pl.multiple_of(1024 + 128 * at_ref[k], 128), 128), :] = refs[k][256:, :]

    return pl.pallas_call(
        kernel,
        in_specs=[SMEM] + [VMEM] * 4 + [ANY] * len(after),
        out_specs=VMEM,
        out_shape=jax.ShapeDtypeStruct((1536, LIVE), BF16),
        compiler_params=params(8),
        cost_estimate=cost(0, 2 << 20),
    )(places, *parts, *after)


def logits_call(groups, stacks, teacher_head, student_head, prior, last):
    n = len(stacks)

    def kernel(at_ref, ht_ref, hs_ref, *refs):
        refs, (ht_buf, hs_buf, x_buf, acc_t, acc_s, old_t, old_s, sem, sum_sem) = refs[:-9], refs[-9:]
        x_refs, refs = refs[:n], refs[n:]
        old = []
        if prior is not None:
            old = [
                pltpu.make_async_copy(refs[0], old_t, sum_sem.at[0]),
                pltpu.make_async_copy(refs[1], old_s, sum_sem.at[1]),
            ]
            refs = refs[2:]
        new = [
            pltpu.make_async_copy(acc_t, refs[0], sum_sem.at[2]),
            pltpu.make_async_copy(acc_s, refs[1], sum_sem.at[3]),
        ]
        fetch_t, fetch_s = [], []
        for k in range(n):
            g = at_ref[k]
            cols_t = pl.ds(pl.multiple_of(1024 * g, 1024), 1024)
            cols_s = pl.ds(pl.multiple_of(512 * g, 512), 512)
            x = x_refs[k]
            fetch_t.append(
                [
                    pltpu.make_async_copy(x.at[pl.ds(0, 1024), :], x_buf.at[k, pl.ds(0, 1024), :], sem.at[k, 0]),
                    pltpu.make_async_copy(
                        ht_ref.at[pl.ds(0, 384), cols_t], ht_buf.at[k, pl.ds(0, 384), :], sem.at[k, 1]
                    ),
                    pltpu.make_async_copy(
                        ht_ref.at[pl.ds(384, 384), cols_t], ht_buf.at[k, pl.ds(384, 384), :], sem.at[k, 2]
                    ),
                ]
            )
            fetch_s.append(
                [
                    pltpu.make_async_copy(x.at[pl.ds(1024, 512), :], x_buf.at[k, pl.ds(1024, 512), :], sem.at[k, 3]),
                    pltpu.make_async_copy(hs_ref.at[:, cols_s], hs_buf.at[k], sem.at[k, 4]),
                ]
            )
            for c in fetch_t[k] + fetch_s[k]:
                c.start()
        for c in old:
            c.start()
        for k in range(n):
            end = k == n - 1
            for c in fetch_t[k]:
                c.wait()
            add_t = jnp.dot(ht_buf[k], x_buf[k, :1024, :], preferred_element_type=F32)
            if end and old:
                old[0].wait()
                add_t += old_t[...]
            if k > 0:
                acc_t[...] += add_t
            else:
                acc_t[...] = add_t
            if end:
                new[0].start()
            for c in fetch_s[k]:
                c.wait()
            add_s = jnp.dot(hs_buf[k], x_buf[k, 1024:, :], preferred_element_type=F32)
            if end and old:
                old[1].wait()
                add_s += old_s[...]
            if k > 0:
                acc_s[...] += add_s
            else:
                acc_s[...] = add_s
        new[1].start()
        if not last:
            refs[2][...] = jnp.zeros((8, 128), F32)
        if last:
            stat_ref, sent_ref = refs[2:]
            t = acc_t[...]
            top_t = jnp.max(t, axis=0, keepdims=True)
            exp_t = jnp.exp(t - top_t)
            sum_t = jnp.sum(exp_t, axis=0, keepdims=True)
            s = acc_s[...]
            cross = jnp.sum(exp_t * (t - s), axis=0, keepdims=True)
            top_s = jnp.max(s, axis=0, keepdims=True)
            sum_s = jnp.sum(jnp.exp(s - top_s), axis=0, keepdims=True)
            lse_t = top_t + jnp.log(sum_t)
            lse_s = top_s + jnp.log(sum_s)
            mean = cross / sum_t
            for j in range(3):
                cols = slice(128 * j, 128 * (j + 1))
                stat_ref[j : j + 1, :] = lse_t[:, cols]
                stat_ref[3 + j : 4 + j, :] = lse_s[:, cols]
                stat_ref[8 + j : 9 + j, :] = mean[:, cols]
            sent_ref[...] = jnp.broadcast_to(stat_ref[:8, :][None], (128, 8, 128))
        for c in new:
            c.wait()

    args = [groups, teacher_head, student_head, *stacks]
    if prior is not None:
        args += list(prior)
    out_shape = [jax.ShapeDtypeStruct((VOC, LIVE), F32)] * 2
    if last:
        out_shape.append(jax.ShapeDtypeStruct((16, 128), F32))
        out_shape.append(jax.ShapeDtypeStruct((128, 8, 128), F32))
    else:
        out_shape.append(jax.ShapeDtypeStruct((8, 128), F32))
    return pl.pallas_call(
        kernel,
        in_specs=[SMEM] + [ANY] * (len(args) - 1),
        out_specs=[ANY, ANY] + [VMEM] * (len(out_shape) - 2),
        out_shape=out_shape,
        scratch_shapes=[
            pltpu.VMEM((n, VOC, 1024), BF16),
            pltpu.VMEM((n, VOC, 512), BF16),
            pltpu.VMEM((n, 1536, LIVE), BF16),
            pltpu.VMEM((VOC, LIVE), F32),
            pltpu.VMEM((VOC, LIVE), F32),
            pltpu.VMEM((VOC, LIVE), F32),
            pltpu.VMEM((VOC, LIVE), F32),
            pltpu.SemaphoreType.DMA((n, 5)),
            pltpu.SemaphoreType.DMA((4,)),
        ],
        compiler_params=params(BIG),
        cost_estimate=cost(n * 2 * 1536 * LIVE * VOC, n * 8 << 20),
    )(*args)


def head_copies(at_ref, h_ref, h_buf, sem):
    return [
        pltpu.make_async_copy(
            h_ref.at[:, pl.ds(pl.multiple_of(512 * at_ref[k], 512), 512)], h_buf.at[k], sem.at[k]
        )
        for k in range(4)
    ]


def logit_grad_call(groups, logits_t, logits_s, stat, all_stats, weight, student_head):
    def kernel(at_ref, t_ref, s_ref, stat_ref, all_ref, w_ref, h_ref, out_ref, g_ref, kl_ref, t_buf, s_buf, h_buf, o_buf, sem, sum_sem, out_sem):
        sums = [
            pltpu.make_async_copy(s_ref, s_buf, sum_sem.at[0]),
            pltpu.make_async_copy(t_ref, t_buf, sum_sem.at[1]),
        ]
        copies = head_copies(at_ref, h_ref, h_buf, sem)
        for c in sums + copies:
            c.start()
        every = all_ref[...]
        top = jnp.max(every, axis=0)
        total = top + jnp.log(jnp.sum(jnp.exp(every - top[None]), axis=0))
        log_zt = jnp.concatenate([total[j : j + 1] for j in range(3)], axis=1)
        log_zs = jnp.concatenate([total[3 + j : 4 + j] for j in range(3)], axis=1)
        own_t = jnp.concatenate([stat_ref[j : j + 1, :] for j in range(3)], axis=1)
        mean = jnp.concatenate([stat_ref[8 + j : 9 + j, :] for j in range(3)], axis=1)
        w = w_ref[...]
        for c in sums:
            c.wait()
        g_ref[...] = (w * (jnp.exp(s_buf[...] - log_zs) - jnp.exp(t_buf[...] - log_zt))).astype(BF16)
        share = jnp.sum(w * mean * jnp.exp(own_t - log_zt), axis=1, keepdims=True)
        common = jnp.sum(w * (log_zs - log_zt), axis=1, keepdims=True)
        kl_ref[0:1, :] = jnp.broadcast_to(share, (1, 128))
        kl_ref[1:2, :] = jnp.broadcast_to(common, (1, 128))
        leave = []
        for k in range(4):
            copies[k].wait()
            o_buf[k] = lax.dot_general(h_buf[k], g_ref[...], TN, preferred_element_type=F32).astype(BF16)
            leave.append(pltpu.make_async_copy(o_buf.at[k], out_ref.at[k], out_sem.at[k]))
            leave[k].start()
        for c in leave:
            c.wait()

    return pl.pallas_call(
        kernel,
        in_specs=[SMEM, ANY, ANY, VMEM, VMEM, VMEM, ANY],
        out_specs=[ANY, VMEM, VMEM],
        scratch_shapes=[
            pltpu.VMEM((VOC, LIVE), F32),
            pltpu.VMEM((VOC, LIVE), F32),
            pltpu.VMEM((4, VOC, 512), BF16),
            pltpu.VMEM((4, 512, LIVE), BF16),
            pltpu.SemaphoreType.DMA((4,)),
            pltpu.SemaphoreType.DMA((2,)),
            pltpu.SemaphoreType.DMA((4,)),
        ],
        out_shape=[
            jax.ShapeDtypeStruct((4, 512, LIVE), BF16),
            jax.ShapeDtypeStruct((VOC, LIVE), BF16),
            jax.ShapeDtypeStruct((8, 128), F32),
        ],
        compiler_params=params(BIG - 4),
        cost_estimate=cost(2 * LIVE * VOC * 2048, 8 << 20, VOC * LIVE * 2),
    )(groups, logits_t, logits_s, stat, all_stats, weight, student_head)


def hidden_half_call(groups, grad, student_head):
    def kernel(at_ref, g_ref, h_ref, out_ref, h_buf, o_buf, sem, out_sem):
        copies = head_copies(at_ref, h_ref, h_buf, sem)
        for c in copies:
            c.start()
        leave = []
        for k in range(4):
            copies[k].wait()
            o_buf[k] = lax.dot_general(h_buf[k], g_ref[...], TN, preferred_element_type=F32)
            leave.append(pltpu.make_async_copy(o_buf.at[k], out_ref.at[k], out_sem.at[k]))
            leave[k].start()
        for c in leave:
            c.wait()

    return pl.pallas_call(
        kernel,
        in_specs=[SMEM, VMEM, ANY],
        out_specs=ANY,
        scratch_shapes=[
            pltpu.VMEM((4, VOC, 512), BF16),
            pltpu.VMEM((4, 512, LIVE), F32),
            pltpu.SemaphoreType.DMA((4,)),
            pltpu.SemaphoreType.DMA((4,)),
        ],
        out_shape=jax.ShapeDtypeStruct((4, 512, LIVE), F32),
        compiler_params=params(BIG - 4),
        cost_estimate=cost(2 * LIVE * VOC * 2048, 7 << 20),
    )(groups, grad, student_head)


def head_grad_call(groups, stacks, grad):
    n = len(stacks)

    def kernel(at_ref, g_ref, *refs):
        out_ref, done_ref, x_buf, held_ref, in_sem, out_sem = refs[n:]
        fetch = [
            pltpu.make_async_copy(refs[k].at[pl.ds(1024, 512), :], x_buf.at[k % 2], in_sem.at[k % 2])
            for k in range(n)
        ]
        store = [
            pltpu.make_async_copy(
                held_ref.at[k % 2],
                out_ref.at[:, pl.ds(pl.multiple_of(512 * at_ref[k], 512), 512)],
                out_sem.at[k % 2],
            )
            for k in range(n)
        ]
        fetch[0].start()
        for k in range(n):
            if k + 1 < n:
                fetch[k + 1].start()
            fetch[k].wait()
            if k >= 2:
                store[k - 2].wait()
            held_ref[k % 2] = lax.dot_general(
                g_ref[...], x_buf[k % 2], NT, preferred_element_type=F32
            ).astype(BF16)
            store[k].start()
        done_ref[...] = jnp.zeros((8, 128), F32)
        store[n - 2].wait()
        store[n - 1].wait()

    return pl.pallas_call(
        kernel,
        in_specs=[SMEM, VMEM] + [ANY] * n,
        out_specs=[ANY, VMEM],
        out_shape=[jax.ShapeDtypeStruct((VOC, DS), BF16), jax.ShapeDtypeStruct((8, 128), F32)],
        scratch_shapes=[
            pltpu.VMEM((2, 512, LIVE), BF16),
            pltpu.VMEM((2, VOC, 512), BF16),
            pltpu.SemaphoreType.DMA((2,)),
            pltpu.SemaphoreType.DMA((2,)),
        ],
        compiler_params=params(BIG - 4),
        cost_estimate=cost(2 * LIVE * VOC * DS, 10 << 20),
    )(groups, grad, *stacks)


def join_call(full, half):
    def kernel(f_ref, h_ref, o1_ref, o2_ref, o3_ref, own_ref, f_buf, buf, f_sem, sem):
        full = [pltpu.make_async_copy(f_ref.at[k], f_buf.at[k], f_sem.at[k]) for k in range(4)]
        copies = [pltpu.make_async_copy(h_ref.at[k], buf.at[k], sem.at[k]) for k in range(4)]
        for k in (1, 2, 3, 0):
            full[k].start()
            copies[k].start()
        for k, o_ref in ((1, o1_ref), (2, o2_ref), (3, o3_ref), (0, own_ref)):
            full[k].wait()
            copies[k].wait()
            o_ref[...] = (f_buf[k] + buf[k].astype(F32)).astype(o_ref.dtype)

    return pl.pallas_call(
        kernel,
        in_specs=[ANY, ANY],
        out_specs=[VMEM] * 4,
        out_shape=[jax.ShapeDtypeStruct((512, LIVE), BF16)] * 3 + [jax.ShapeDtypeStruct((512, LIVE), F32)],
        scratch_shapes=[
            pltpu.VMEM((4, 512, LIVE), F32),
            pltpu.VMEM((4, 512, LIVE), BF16),
            pltpu.SemaphoreType.DMA((4,)),
            pltpu.SemaphoreType.DMA((4,)),
        ],
        compiler_params=params(16),
        cost_estimate=cost(0, 8 << 20),
    )(full, half)


def sum_major_call(at, own, came, after):
    def kernel(at_ref, own_ref, c0, c1, c2, after_ref, *refs):
        outs, (buf, sem) = refs[:4], refs[4:]
        copies = [pltpu.make_async_copy(c, buf.at[k], sem.at[k]) for k, c in enumerate((c0, c1, c2))]
        for c in copies:
            c.start()
        for c in copies:
            c.wait()
        for l in (1, 2, 3, 0):
            rows = pl.ds(pl.multiple_of(128 * at_ref[l], 128), 128)
            total = own_ref[rows, :]
            for k in range(3):
                total += buf[k, rows, :].astype(F32)
            outs[l][...] = total

    return pl.pallas_call(
        kernel,
        in_specs=[SMEM, VMEM, ANY, ANY, ANY, ANY],
        out_specs=[VMEM] * 4,
        out_shape=[jax.ShapeDtypeStruct((128, LIVE), F32)] * 4,
        scratch_shapes=[pltpu.VMEM((3, 512, LIVE), BF16), pltpu.SemaphoreType.DMA((3,))],
        compiler_params=params(16),
        cost_estimate=cost(0, 4 << 20),
    )(at, own, *came, after)


def return_call(slot, own, came, kl):
    def kernel(slot_ref, own_ref, c0, c1, c2, kl_ref, out_ref, buf, sem):
        copies = [pltpu.make_async_copy(c, buf.at[k], sem.at[k]) for k, c in enumerate((c0, c1, c2))]
        for c in copies:
            c.start()
        share = kl_ref[0:1, :]
        hi = share.astype(BF16).astype(F32)
        mid = (share - hi).astype(BF16).astype(F32)
        low = share - hi - mid
        lane = lax.broadcasted_iota(jnp.int32, (1, 128), 1)
        extra = jnp.where(lane == 0, hi, jnp.where(lane == 1, mid, jnp.where(lane == 2, low, 0.0)))
        extra = jnp.broadcast_to(extra, (256, 128))
        row = lax.broadcasted_iota(jnp.int32, (256, LIVE), 0)
        eighth = lax.broadcasted_iota(jnp.int32, (256, 128), 0) % 8 == 7
        total = own_ref[...]
        for k in range(3):
            copies[k].wait()
            total += buf[k]
        total = total.astype(BF16)
        for j in range(4):
            pick = jnp.where(row + 256 * j == slot_ref[...], 1.0, 0.0).astype(BF16)
            back = lax.dot_general(pick, total, NT, preferred_element_type=F32)
            back = jnp.where(eighth, extra, back)
            out_ref[32 * j : 32 * (j + 1)] = back.reshape(32, 8, 128).astype(BF16)

    return pl.pallas_call(
        kernel,
        in_specs=[VMEM, VMEM, ANY, ANY, ANY, VMEM],
        out_specs=VMEM,
        out_shape=jax.ShapeDtypeStruct((128, 8, 128), BF16),
        scratch_shapes=[pltpu.VMEM((3, 128, LIVE), F32), pltpu.SemaphoreType.DMA((3,))],
        compiler_params=params(16),
        cost_estimate=cost(2 * 1024 * LIVE * 128, 2 << 20),
    )(slot, own, *came, kl)


def collect_call(back, kl):
    def kernel(b_ref, kl_ref, out_ref, mean_ref):
        shares = jnp.zeros((8, 128), F32)
        for y in range(4):
            for c in range(2):
                for x in range(4):
                    u = unit_of(y, c, x)
                    total = sum(b_ref[flat(y, c, x, z)].astype(F32) for z in range(4))
                    shares += total
                    out_ref[:, 128 * u : 128 * (u + 1)] = total.astype(BF16)[:OWN]
        row = lax.broadcasted_iota(jnp.int32, (8, 128), 0)
        lane = lax.broadcasted_iota(jnp.int32, (8, 128), 1)
        shares = jnp.where((row == 7) & (lane < 3), shares, 0.0)
        mean_ref[0, 0] = (jnp.sum(shares) + kl_ref[1, 0]) / LIVE

    return pl.pallas_call(
        kernel,
        in_specs=[VMEM, SMEM],
        out_specs=[VMEM, SMEM],
        out_shape=[jax.ShapeDtypeStruct((OWN, DS), BF16), jax.ShapeDtypeStruct((1, 1), F32)],
        compiler_params=params(8),
        cost_estimate=cost(0, 1 << 20),
    )(back, kl)


def local(student_hidden, teacher_hidden, student_head, teacher_head, token_weight, block_count):
    me = lax.axis_index("dp") * 16 + lax.axis_index("vocab")
    y, core, x, z = me // 32, (me // 16) % 2, (me // 4) % 4, me % 4
    turn = jnp.arange(4, dtype=jnp.int32)
    major_at = jnp.where(core == 0, y, x)
    minor_at = jnp.where(core == 0, x, y)

    arrived = lax.all_to_all(
        spread_call(teacher_hidden, student_hidden, token_weight), AXES, split_axis=0, concat_axis=0, tiled=True
    )

    ends = jnp.cumsum(block_count)
    block = jnp.arange(LIVE, dtype=jnp.int32) // BLOCK
    shard = jnp.sum((block[:, None] >= ends[None, :]).astype(jnp.int32), axis=1)
    begin = jnp.sum(jnp.where(jnp.arange(8)[None, :] < shard[:, None], block_count[None, :], 0), axis=1)
    place = (block - begin) * BLOCK + jnp.arange(LIVE, dtype=jnp.int32) % BLOCK
    slot = (shard * 16 + place // OWN) * 8 + place % OWN
    slots = jnp.arange(1024, dtype=jnp.int32)
    pick = (slot[:, None] == slots[None, :]).astype(BF16)
    own = lax.dot_general(
        arrived.reshape(1024, LIVE), pick, (((0,), (1,)), ((), ())), preferred_element_type=F32
    ).astype(BF16)
    weight = lax.dot_general(arrived[:, 7, :8].reshape(1, 1024), pick, NT, preferred_element_type=F32)

    piece = permute(own, across())
    parts = [own] + [permute(own, minor(l)) for l in (1, 2, 3)]
    heads = (teacher_head, student_head)
    stack = assemble_call((minor_at - turn + 4) % 4, parts, (piece,))
    before, after = permute(stack, major(1)), permute(stack, major(3))
    sib_stack = permute(stack, SWAP)
    pieces = [piece] + [permute(piece, along_z(l)) for l in (1, 2, 3)]

    def groups(*steps):
        steps = jnp.array(steps, jnp.int32)
        mine = core * 4 + (major_at - steps + 4) % 4
        theirs = (1 - core) * 4 + (minor_at - steps + 4) % 4
        return mine, theirs

    mine, theirs = groups(0)
    *sums, begun = logits_call(jnp.concatenate([mine, theirs]), [stack, sib_stack], *heads, None, False)
    before, after, begun = lax.optimization_barrier((before, after, begun))
    opposite = assemble_call((minor_at + z - turn + 4) % 4, pieces, [begun])
    sib_before, sib_after, sib_opposite = (permute(s, SWAP) for s in (before, after, opposite))
    mine, theirs = groups(1, 3, 2)
    *sums, _ = logits_call(mine, [before, after, opposite], *heads, sums, False)
    logits_t, logits_s, stat, sent = logits_call(
        theirs, [sib_before, sib_after, sib_opposite], *heads, sums, True
    )
    all_stats = lax.all_to_all(sent, AXES, split_axis=0, concat_axis=0, tiled=True)

    half, grad, kl = logit_grad_call(
        (1 - core) * 4 + (minor_at + turn) % 4, logits_t, logits_s, stat, all_stats, weight, heads[1]
    )
    half = permute(half, SWAP)
    full = hidden_half_call(core * 4 + (major_at + turn) % 4, grad, heads[1])
    mine, theirs = groups(0, 1, 2, 3)
    head_grad, done = head_grad_call(
        jnp.concatenate([mine, theirs]),
        [stack, before, opposite, after, sib_stack, sib_before, sib_opposite, sib_after],
        grad,
    )

    *leave, kept = join_call(full, half)
    came = [permute(leave[k - 1], major(k)) for k in (1, 2, 3)]
    kept, *leave = sum_major_call((minor_at + turn) % 4, kept, came, done)
    came = [permute(leave[l - 1], minor(l)) for l in (1, 2, 3)]
    back = return_call(slot.reshape(1, LIVE), kept, came, kl)
    back = lax.all_to_all(back, AXES, split_axis=0, concat_axis=0, tiled=True)
    hidden_grad, kl_mean = collect_call(back, kl)
    return kl_mean.reshape(()), hidden_grad, head_grad


def solution(mesh):
    rows = P(AXES, None)
    return jax.shard_map(
        local,
        mesh=mesh,
        in_specs=(rows, rows, rows, rows, P(AXES), P()),
        out_specs=(P(), rows, rows),
        check_vma=False,
    )
```

```python
import jax
import jax.numpy as jnp
from jax import lax
from jax.experimental import pallas as pl
from jax.experimental.pallas import tpu as pltpu
from jax.sharding import PartitionSpec as P

BLOCK = 16
LIVE = 384
OWN = 7
VOC = 768
DT = 8192
DS = 4096
AXES = ("dp", "vocab")
F32 = jnp.float32
BF16 = jnp.bfloat16
NT = (((1,), (1,)), ((), ()))
TN = (((0,), (0,)), ((), ()))


def flat(y, c, x, z):
    return ((y * 2 + c) * 4 + x) * 4 + z


def perm_of(move):
    return [
        (flat(y, c, x, z), flat(*move(y, c, x, z)))
        for y in range(4)
        for c in range(2)
        for x in range(4)
        for z in range(4)
    ]


def minor(shift):
    return perm_of(
        lambda y, c, x, z: (y, c, (x + shift) % 4, z) if c == 0 else ((y + shift) % 4, c, x, z)
    )


def major(shift):
    return perm_of(
        lambda y, c, x, z: ((y + shift) % 4, c, x, z) if c == 0 else (y, c, (x + shift) % 4, z)
    )


def along_z(shift):
    return perm_of(lambda y, c, x, z: (y, c, x, (z + shift) % 4))


def across():
    return perm_of(
        lambda y, c, x, z: ((y + 2) % 4, c, (x - z) % 4, z) if c == 0 else ((y - z) % 4, c, (x + 2) % 4, z)
    )


SWAP = perm_of(lambda y, c, x, z: (y, 1 - c, x, z))


def permute(value, pairs):
    return lax.ppermute(value, AXES, pairs)


def unit_of(y, c, x):
    return y * 4 + x if c == 0 else 16 + x * 4 + y


BIG = 56
SMEM = pl.BlockSpec(memory_space=pltpu.SMEM)
VMEM = pl.BlockSpec(memory_space=pltpu.VMEM)
HBM = pl.BlockSpec(memory_space=pltpu.HBM)
ANY = pl.BlockSpec(memory_space=pl.ANY)


def params(limit_mib):
    return pltpu.CompilerParams(vmem_limit_bytes=limit_mib * 1024 * 1024)


def cost(flops, nbytes, transcendentals=0):
    return pl.CostEstimate(flops=flops, bytes_accessed=nbytes, transcendentals=transcendentals)


def spread_call(teacher_hidden, student_hidden, token_weight):
    def kernel(t_ref, s_ref, w_ref, out_ref):
        w = jnp.pad(w_ref[...].astype(F32), ((0, 0), (0, 256 - OWN)))
        none = jnp.zeros((1, 128), F32)
        for y in range(4):
            for c in range(2):
                for x in range(4):
                    u = unit_of(y, c, x)
                    t = t_ref[:, 256 * u : 256 * (u + 1)].astype(F32)
                    s = s_ref[:, 128 * u : 128 * (u + 1)].astype(F32)
                    t = jnp.concatenate([t, w], axis=0).astype(BF16)
                    s = jnp.concatenate([s, none], axis=0).astype(BF16)
                    for z in range(4):
                        out_ref[flat(y, c, x, z), :, :256] = t
                        out_ref[flat(y, c, x, z), :, 256:] = s

    return pl.pallas_call(
        kernel,
        grid=(1,),
        in_specs=[
            pl.BlockSpec((OWN, DT), lambda i: (0, 0)),
            pl.BlockSpec((OWN, DS), lambda i: (0, 0)),
            pl.BlockSpec((1, OWN), lambda i: (0, 0)),
        ],
        out_specs=pl.BlockSpec((128, 8, LIVE), lambda i: (0, 0, 0)),
        out_shape=jax.ShapeDtypeStruct((128, 8, LIVE), BF16),
        compiler_params=params(BIG),
        cost_estimate=cost(0, 1 << 20),
    )(teacher_hidden, student_hidden, token_weight.reshape(1, OWN))


def assemble_call(places, parts, after):
    def kernel(at_ref, *refs):
        out_ref = refs[-1]
        for k in range(4):
            out_ref[pl.ds(pl.multiple_of(256 * at_ref[k], 256), 256), :] = refs[k][:256, :]
            out_ref[pl.ds(pl.multiple_of(1024 + 128 * at_ref[k], 128), 128), :] = refs[k][256:, :]

    return pl.pallas_call(
        kernel,
        in_specs=[SMEM] + [VMEM] * 4 + [ANY] * len(after),
        out_specs=VMEM,
        out_shape=jax.ShapeDtypeStruct((1536, LIVE), BF16),
        compiler_params=params(8),
        cost_estimate=cost(0, 2 << 20),
    )(places, *parts, *after)


def hold_call(values, after):
    n = len(values)

    def kernel(*refs):
        pass

    return pl.pallas_call(
        kernel,
        in_specs=[ANY] * (n + len(after)),
        out_specs=[ANY] * n,
        out_shape=[jax.ShapeDtypeStruct(v.shape, v.dtype) for v in values],
        input_output_aliases={k: k for k in range(n)},
        compiler_params=params(50),
        cost_estimate=cost(0, 0),
    )(*values, *after)


def logits_call(groups, stacks, teacher_head, student_head, prior, last):
    n = len(stacks)

    def kernel(at_ref, ht_ref, hs_ref, *refs):
        refs, (ht_buf, hs_buf, x_buf, sem) = refs[:-4], refs[-4:]
        x_refs, refs = refs[:n], refs[n:]
        if prior is not None:
            old_t, old_s, *refs = refs
        acc_t, acc_s = refs[:2]
        fetch_t, fetch_s = [], []
        for k in range(n):
            g = at_ref[k]
            cols_t = pl.ds(pl.multiple_of(1024 * g, 1024), 1024)
            cols_s = pl.ds(pl.multiple_of(512 * g, 512), 512)
            x = x_refs[k]
            fetch_t.append(
                [
                    pltpu.make_async_copy(x.at[pl.ds(0, 1024), :], x_buf.at[k, pl.ds(0, 1024), :], sem.at[k, 0]),
                    pltpu.make_async_copy(
                        ht_ref.at[pl.ds(0, 384), cols_t], ht_buf.at[k, pl.ds(0, 384), :], sem.at[k, 1]
                    ),
                    pltpu.make_async_copy(
                        ht_ref.at[pl.ds(384, 384), cols_t], ht_buf.at[k, pl.ds(384, 384), :], sem.at[k, 2]
                    ),
                ]
            )
            fetch_s.append(
                [
                    pltpu.make_async_copy(x.at[pl.ds(1024, 512), :], x_buf.at[k, pl.ds(1024, 512), :], sem.at[k, 3]),
                    pltpu.make_async_copy(hs_ref.at[:, cols_s], hs_buf.at[k], sem.at[k, 4]),
                ]
            )
            for c in fetch_t[k] + fetch_s[k]:
                c.start()
        for k in range(n):
            for c in fetch_t[k]:
                c.wait()
            add_t = jnp.dot(ht_buf[k], x_buf[k, :1024, :], preferred_element_type=F32)
            if k > 0:
                acc_t[...] += add_t
            elif prior is None:
                acc_t[...] = add_t
            else:
                acc_t[...] = old_t[...] + add_t
            for c in fetch_s[k]:
                c.wait()
            add_s = jnp.dot(hs_buf[k], x_buf[k, 1024:, :], preferred_element_type=F32)
            if k > 0:
                acc_s[...] += add_s
            elif prior is None:
                acc_s[...] = add_s
            else:
                acc_s[...] = old_s[...] + add_s
        if not last:
            refs[2][...] = jnp.zeros((8, 128), F32)
        if last:
            stat_ref, sent_ref = refs[2:]
            t = acc_t[...]
            top_t = jnp.max(t, axis=0, keepdims=True)
            exp_t = jnp.exp(t - top_t)
            sum_t = jnp.sum(exp_t, axis=0, keepdims=True)
            s = acc_s[...]
            cross = jnp.sum(exp_t * (t - s), axis=0, keepdims=True)
            top_s = jnp.max(s, axis=0, keepdims=True)
            sum_s = jnp.sum(jnp.exp(s - top_s), axis=0, keepdims=True)
            lse_t = top_t + jnp.log(sum_t)
            lse_s = top_s + jnp.log(sum_s)
            mean = cross / sum_t
            for j in range(3):
                cols = slice(128 * j, 128 * (j + 1))
                stat_ref[j : j + 1, :] = lse_t[:, cols]
                stat_ref[3 + j : 4 + j, :] = lse_s[:, cols]
                stat_ref[8 + j : 9 + j, :] = mean[:, cols]
            sent_ref[...] = jnp.broadcast_to(stat_ref[:8, :][None], (128, 8, 128))

    args = [groups, teacher_head, student_head, *stacks]
    if prior is not None:
        args += list(prior)
    out_shape = [jax.ShapeDtypeStruct((VOC, LIVE), F32)] * 2
    if last:
        out_shape.append(jax.ShapeDtypeStruct((16, 128), F32))
        out_shape.append(jax.ShapeDtypeStruct((128, 8, 128), F32))
    else:
        out_shape.append(jax.ShapeDtypeStruct((8, 128), F32))
    return pl.pallas_call(
        kernel,
        in_specs=[SMEM] + [ANY] * (n + 2) + [VMEM] * (len(args) - 3 - n),
        out_specs=[VMEM] * len(out_shape),
        out_shape=out_shape,
        input_output_aliases={} if prior is None else {3 + n: 0, 4 + n: 1},
        scratch_shapes=[
            pltpu.VMEM((n, VOC, 1024), BF16),
            pltpu.VMEM((n, VOC, 512), BF16),
            pltpu.VMEM((n, 1536, LIVE), BF16),
            pltpu.SemaphoreType.DMA((n, 5)),
        ],
        compiler_params=params(50),
        cost_estimate=cost(n * 2 * 1536 * LIVE * VOC, n * 8 << 20),
    )(*args)


def logit_grad_call(groups, logits_t, logits_s, stat, all_stats, weight, student_head):
    def kernel(at_ref, t_ref, s_ref, stat_ref, all_ref, w_ref, h_ref, out_ref, g_ref, kl_ref):
        every = all_ref[...]
        top = jnp.max(every, axis=0)
        total = top + jnp.log(jnp.sum(jnp.exp(every - top[None]), axis=0))
        log_zt = jnp.concatenate([total[j : j + 1] for j in range(3)], axis=1)
        log_zs = jnp.concatenate([total[3 + j : 4 + j] for j in range(3)], axis=1)
        own_t = jnp.concatenate([stat_ref[j : j + 1, :] for j in range(3)], axis=1)
        mean = jnp.concatenate([stat_ref[8 + j : 9 + j, :] for j in range(3)], axis=1)
        w = w_ref[...]
        g_ref[...] = (w * (jnp.exp(s_ref[...] - log_zs) - jnp.exp(t_ref[...] - log_zt))).astype(BF16)
        share = jnp.sum(w * mean * jnp.exp(own_t - log_zt), axis=1, keepdims=True)
        common = jnp.sum(w * (log_zs - log_zt), axis=1, keepdims=True)
        kl_ref[0:1, :] = jnp.broadcast_to(share, (1, 128))
        kl_ref[1:2, :] = jnp.broadcast_to(common, (1, 128))
        for k in range(4):
            head = h_ref[:, pl.ds(pl.multiple_of(512 * at_ref[k], 512), 512)]
            out_ref[k] = lax.dot_general(head, g_ref[...], TN, preferred_element_type=F32).astype(BF16)

    return pl.pallas_call(
        kernel,
        in_specs=[SMEM] + [VMEM] * 6,
        out_specs=[VMEM] * 3,
        out_shape=[
            jax.ShapeDtypeStruct((4, 512, LIVE), BF16),
            jax.ShapeDtypeStruct((VOC, LIVE), BF16),
            jax.ShapeDtypeStruct((8, 128), F32),
        ],
        compiler_params=params(16),
        cost_estimate=cost(2 * LIVE * VOC * 2048, 8 << 20, VOC * LIVE * 2),
    )(groups, logits_t, logits_s, stat, all_stats, weight, student_head)


def hidden_half_call(groups, grad, student_head):
    def kernel(at_ref, g_ref, h_ref, out_ref):
        for k in range(4):
            head = h_ref[:, pl.ds(pl.multiple_of(512 * at_ref[k], 512), 512)]
            out_ref[k] = lax.dot_general(head, g_ref[...], TN, preferred_element_type=F32)

    return pl.pallas_call(
        kernel,
        in_specs=[SMEM, VMEM, VMEM],
        out_specs=VMEM,
        out_shape=jax.ShapeDtypeStruct((4, 512, LIVE), F32),
        compiler_params=params(16),
        cost_estimate=cost(2 * LIVE * VOC * 2048, 7 << 20),
    )(groups, grad, student_head)


def head_grad_call(groups, stacks, grad):
    n = len(stacks)

    def kernel(at_ref, g_ref, *refs):
        out_ref, done_ref, x_buf, held_ref, in_sem, out_sem = refs[n:]
        fetch = [
            pltpu.make_async_copy(refs[k].at[pl.ds(1024, 512), :], x_buf.at[k % 2], in_sem.at[k % 2])
            for k in range(n)
        ]
        store = [
            pltpu.make_async_copy(
                held_ref.at[k % 2],
                out_ref.at[:, pl.ds(pl.multiple_of(512 * at_ref[k], 512), 512)],
                out_sem.at[k % 2],
            )
            for k in range(n)
        ]
        fetch[0].start()
        for k in range(n):
            if k + 1 < n:
                fetch[k + 1].start()
            fetch[k].wait()
            if k >= 2:
                store[k - 2].wait()
            held_ref[k % 2] = lax.dot_general(
                g_ref[...], x_buf[k % 2], NT, preferred_element_type=F32
            ).astype(BF16)
            store[k].start()
        done_ref[...] = jnp.zeros((8, 128), F32)
        store[n - 2].wait()
        store[n - 1].wait()

    return pl.pallas_call(
        kernel,
        in_specs=[SMEM, VMEM] + [ANY] * n,
        out_specs=[ANY, VMEM],
        out_shape=[jax.ShapeDtypeStruct((VOC, DS), BF16), jax.ShapeDtypeStruct((8, 128), F32)],
        scratch_shapes=[
            pltpu.VMEM((2, 512, LIVE), BF16),
            pltpu.VMEM((2, VOC, 512), BF16),
            pltpu.SemaphoreType.DMA((2,)),
            pltpu.SemaphoreType.DMA((2,)),
        ],
        compiler_params=params(BIG - 4),
        cost_estimate=cost(2 * LIVE * VOC * DS, 10 << 20),
    )(groups, grad, *stacks)


def join_call(full, half):
    def kernel(f_ref, h_ref, o1_ref, o2_ref, o3_ref, own_ref, f_buf, buf, f_sem, sem):
        full = [pltpu.make_async_copy(f_ref.at[k], f_buf.at[k], f_sem.at[k]) for k in range(4)]
        copies = [pltpu.make_async_copy(h_ref.at[k], buf.at[k], sem.at[k]) for k in range(4)]
        for k in (1, 2, 3, 0):
            full[k].start()
            copies[k].start()
        for k, o_ref in ((1, o1_ref), (2, o2_ref), (3, o3_ref), (0, own_ref)):
            full[k].wait()
            copies[k].wait()
            o_ref[...] = (f_buf[k] + buf[k].astype(F32)).astype(o_ref.dtype)

    return pl.pallas_call(
        kernel,
        in_specs=[ANY, ANY],
        out_specs=[VMEM] * 4,
        out_shape=[jax.ShapeDtypeStruct((512, LIVE), BF16)] * 3 + [jax.ShapeDtypeStruct((512, LIVE), F32)],
        scratch_shapes=[
            pltpu.VMEM((4, 512, LIVE), F32),
            pltpu.VMEM((4, 512, LIVE), BF16),
            pltpu.SemaphoreType.DMA((4,)),
            pltpu.SemaphoreType.DMA((4,)),
        ],
        compiler_params=params(16),
        cost_estimate=cost(0, 8 << 20),
    )(full, half)


def sum_major_call(at, own, came, after):
    def kernel(at_ref, own_ref, c0, c1, c2, after_ref, *refs):
        outs, (buf, sem) = refs[:4], refs[4:]
        copies = [pltpu.make_async_copy(c, buf.at[k], sem.at[k]) for k, c in enumerate((c0, c1, c2))]
        for c in copies:
            c.start()
        for c in copies:
            c.wait()
        for l in (1, 2, 3, 0):
            rows = pl.ds(pl.multiple_of(128 * at_ref[l], 128), 128)
            total = own_ref[rows, :]
            for k in range(3):
                total += buf[k, rows, :].astype(F32)
            outs[l][...] = total.astype(outs[l].dtype)

    return pl.pallas_call(
        kernel,
        in_specs=[SMEM, VMEM, ANY, ANY, ANY, ANY],
        out_specs=[VMEM] * 4,
        out_shape=[jax.ShapeDtypeStruct((128, LIVE), F32)] + [jax.ShapeDtypeStruct((128, LIVE), BF16)] * 3,
        scratch_shapes=[pltpu.VMEM((3, 512, LIVE), BF16), pltpu.SemaphoreType.DMA((3,))],
        compiler_params=params(16),
        cost_estimate=cost(0, 4 << 20),
    )(at, own, *came, after)


def return_call(slot, own, came, kl):
    def kernel(slot_ref, own_ref, c0, c1, c2, kl_ref, out_ref, buf, sem):
        copies = [pltpu.make_async_copy(c, buf.at[k], sem.at[k]) for k, c in enumerate((c0, c1, c2))]
        for c in copies:
            c.start()
        share = kl_ref[0:1, :]
        hi = share.astype(BF16).astype(F32)
        mid = (share - hi).astype(BF16).astype(F32)
        low = share - hi - mid
        lane = lax.broadcasted_iota(jnp.int32, (1, 128), 1)
        extra = jnp.where(lane == 0, hi, jnp.where(lane == 1, mid, jnp.where(lane == 2, low, 0.0)))
        extra = jnp.broadcast_to(extra, (256, 128))
        row = lax.broadcasted_iota(jnp.int32, (256, LIVE), 0)
        eighth = lax.broadcasted_iota(jnp.int32, (256, 128), 0) % 8 == 7
        total = own_ref[...]
        for k in range(3):
            copies[k].wait()
            total += buf[k].astype(F32)
        total = total.astype(BF16)
        for j in range(4):
            pick = jnp.where(row + 256 * j == slot_ref[...], 1.0, 0.0).astype(BF16)
            back = lax.dot_general(pick, total, NT, preferred_element_type=F32)
            back = jnp.where(eighth, extra, back)
            out_ref[32 * j : 32 * (j + 1)] = back.reshape(32, 8, 128).astype(BF16)

    return pl.pallas_call(
        kernel,
        in_specs=[VMEM, VMEM, ANY, ANY, ANY, VMEM],
        out_specs=VMEM,
        out_shape=jax.ShapeDtypeStruct((128, 8, 128), BF16),
        scratch_shapes=[pltpu.VMEM((3, 128, LIVE), BF16), pltpu.SemaphoreType.DMA((3,))],
        compiler_params=params(16),
        cost_estimate=cost(2 * 1024 * LIVE * 128, 2 << 20),
    )(slot, own, *came, kl)


def collect_call(back, kl):
    def kernel(b_ref, kl_ref, out_ref, mean_ref):
        shares = jnp.zeros((8, 128), F32)
        for y in range(4):
            for c in range(2):
                for x in range(4):
                    u = unit_of(y, c, x)
                    total = sum(b_ref[flat(y, c, x, z)].astype(F32) for z in range(4))
                    shares += total
                    out_ref[:, 128 * u : 128 * (u + 1)] = total.astype(BF16)[:OWN]
        row = lax.broadcasted_iota(jnp.int32, (8, 128), 0)
        lane = lax.broadcasted_iota(jnp.int32, (8, 128), 1)
        shares = jnp.where((row == 7) & (lane < 3), shares, 0.0)
        mean_ref[0, 0] = (jnp.sum(shares) + kl_ref[1, 0]) / LIVE

    return pl.pallas_call(
        kernel,
        in_specs=[VMEM, SMEM],
        out_specs=[VMEM, SMEM],
        out_shape=[jax.ShapeDtypeStruct((OWN, DS), BF16), jax.ShapeDtypeStruct((1, 1), F32)],
        compiler_params=params(8),
        cost_estimate=cost(0, 1 << 20),
    )(back, kl)


def local(student_hidden, teacher_hidden, student_head, teacher_head, token_weight, block_count):
    me = lax.axis_index("dp") * 16 + lax.axis_index("vocab")
    y, core, x, z = me // 32, (me // 16) % 2, (me // 4) % 4, me % 4
    turn = jnp.arange(4, dtype=jnp.int32)
    major_at = jnp.where(core == 0, y, x)
    minor_at = jnp.where(core == 0, x, y)

    arrived = lax.all_to_all(
        spread_call(teacher_hidden, student_hidden, token_weight), AXES, split_axis=0, concat_axis=0, tiled=True
    )

    ends = jnp.cumsum(block_count)
    block = jnp.arange(LIVE, dtype=jnp.int32) // BLOCK
    shard = jnp.sum((block[:, None] >= ends[None, :]).astype(jnp.int32), axis=1)
    begin = jnp.sum(jnp.where(jnp.arange(8)[None, :] < shard[:, None], block_count[None, :], 0), axis=1)
    place = (block - begin) * BLOCK + jnp.arange(LIVE, dtype=jnp.int32) % BLOCK
    slot = (shard * 16 + place // OWN) * 8 + place % OWN
    slots = jnp.arange(1024, dtype=jnp.int32)
    pick = (slot[:, None] == slots[None, :]).astype(BF16)
    own = lax.dot_general(
        arrived.reshape(1024, LIVE), pick, (((0,), (1,)), ((), ())), preferred_element_type=F32
    ).astype(BF16)
    weight = lax.dot_general(arrived[:, 7, :8].reshape(1, 1024), pick, NT, preferred_element_type=F32)

    piece = permute(own, across())
    parts = [own] + [permute(own, minor(l)) for l in (1, 2, 3)]
    heads = (teacher_head, student_head)
    stack = assemble_call((minor_at - turn + 4) % 4, parts, (piece,))
    before, after = permute(stack, major(1)), permute(stack, major(3))
    sib_stack = permute(stack, SWAP)
    pieces = [piece] + [permute(piece, along_z(l)) for l in (1, 2, 3)]

    def groups(*steps):
        steps = jnp.array(steps, jnp.int32)
        mine = core * 4 + (major_at - steps + 4) % 4
        theirs = (1 - core) * 4 + (minor_at - steps + 4) % 4
        return mine, theirs

    mine, theirs = groups(0)
    *sums, token = logits_call(jnp.concatenate([mine, theirs]), [stack, sib_stack], *heads, None, False)
    opposite = assemble_call((minor_at + z - turn + 4) % 4, pieces, [token])
    before, after = hold_call([before, after], [token])
    sib_before, sib_after, sib_opposite = (permute(s, SWAP) for s in (before, after, opposite))
    mine, theirs = groups(1, 3)
    *sums, _ = logits_call(mine, [before, after], *heads, sums, False)
    logits_t, logits_s, stat, sent = logits_call(
        jnp.concatenate([theirs, *groups(2)]), [sib_before, sib_after, opposite, sib_opposite], *heads, sums, True
    )
    all_stats = lax.all_to_all(sent, AXES, split_axis=0, concat_axis=0, tiled=True)

    half, grad, kl = logit_grad_call(
        (1 - core) * 4 + (minor_at + turn) % 4, logits_t, logits_s, stat, all_stats, weight, heads[1]
    )
    half = permute(half, SWAP)
    full = hidden_half_call(core * 4 + (major_at + turn) % 4, grad, heads[1])
    mine, theirs = groups(0, 1, 2, 3)
    head_grad, done = head_grad_call(
        jnp.concatenate([mine, theirs]),
        [stack, before, opposite, after, sib_stack, sib_before, sib_opposite, sib_after],
        grad,
    )

    *leave, kept = join_call(full, half)
    came = [permute(leave[k - 1], major(k)) for k in (1, 2, 3)]
    kept, *leave = sum_major_call((minor_at + turn) % 4, kept, came, done)
    came = [permute(leave[l - 1], minor(l)) for l in (1, 2, 3)]
    back = return_call(slot.reshape(1, LIVE), kept, came, kl)
    back = lax.all_to_all(back, AXES, split_axis=0, concat_axis=0, tiled=True)
    hidden_grad, kl_mean = collect_call(back, kl)
    return kl_mean.reshape(()), hidden_grad, head_grad


def solution(mesh):
    rows = P(AXES, None)
    return jax.shard_map(
        local,
        mesh=mesh,
        in_specs=(rows, rows, rows, rows, P(AXES), P()),
        out_specs=(P(), rows, rows),
        check_vma=False,
    )
```

```python
import jax
import jax.numpy as jnp
from jax import lax
from jax.experimental import pallas as pl
from jax.experimental.pallas import tpu as pltpu
from jax.sharding import PartitionSpec as P

BLOCK = 16
LIVE = 384
OWN = 7
VOC = 768
DT = 8192
DS = 4096
AXES = ("dp", "vocab")
F32 = jnp.float32
BF16 = jnp.bfloat16
NT = (((1,), (1,)), ((), ()))
TN = (((0,), (0,)), ((), ()))


def flat(y, c, x, z):
    return ((y * 2 + c) * 4 + x) * 4 + z


def perm_of(move):
    return [
        (flat(y, c, x, z), flat(*move(y, c, x, z)))
        for y in range(4)
        for c in range(2)
        for x in range(4)
        for z in range(4)
    ]


def minor(shift):
    return perm_of(
        lambda y, c, x, z: (y, c, (x + shift) % 4, z) if c == 0 else ((y + shift) % 4, c, x, z)
    )


def major(shift):
    return perm_of(
        lambda y, c, x, z: ((y + shift) % 4, c, x, z) if c == 0 else (y, c, (x + shift) % 4, z)
    )


def along_z(shift):
    return perm_of(lambda y, c, x, z: (y, c, x, (z + shift) % 4))


def across():
    return perm_of(
        lambda y, c, x, z: ((y + 2) % 4, c, (x - z) % 4, z) if c == 0 else ((y - z) % 4, c, (x + 2) % 4, z)
    )


SWAP = perm_of(lambda y, c, x, z: (y, 1 - c, x, z))


def permute(value, pairs):
    return lax.ppermute(value, AXES, pairs)


def unit_of(y, c, x):
    return y * 4 + x if c == 0 else 16 + x * 4 + y


BIG = 56
SMEM = pl.BlockSpec(memory_space=pltpu.SMEM)
VMEM = pl.BlockSpec(memory_space=pltpu.VMEM)
HBM = pl.BlockSpec(memory_space=pltpu.HBM)
ANY = pl.BlockSpec(memory_space=pl.ANY)


def params(limit_mib):
    return pltpu.CompilerParams(vmem_limit_bytes=limit_mib * 1024 * 1024)


def cost(flops, nbytes, transcendentals=0):
    return pl.CostEstimate(flops=flops, bytes_accessed=nbytes, transcendentals=transcendentals)


def spread_call(teacher_hidden, student_hidden, token_weight):
    def kernel(t_ref, s_ref, w_ref, out_ref):
        w = jnp.pad(w_ref[...].astype(F32), ((0, 0), (0, 256 - OWN)))
        none = jnp.zeros((1, 128), F32)
        for y in range(4):
            for c in range(2):
                for x in range(4):
                    u = unit_of(y, c, x)
                    t = t_ref[:, 256 * u : 256 * (u + 1)].astype(F32)
                    s = s_ref[:, 128 * u : 128 * (u + 1)].astype(F32)
                    t = jnp.concatenate([t, w], axis=0).astype(BF16)
                    s = jnp.concatenate([s, none], axis=0).astype(BF16)
                    for z in range(4):
                        out_ref[flat(y, c, x, z), :, :256] = t
                        out_ref[flat(y, c, x, z), :, 256:] = s

    return pl.pallas_call(
        kernel,
        grid=(1,),
        in_specs=[
            pl.BlockSpec((OWN, DT), lambda i: (0, 0)),
            pl.BlockSpec((OWN, DS), lambda i: (0, 0)),
            pl.BlockSpec((1, OWN), lambda i: (0, 0)),
        ],
        out_specs=pl.BlockSpec((128, 8, LIVE), lambda i: (0, 0, 0)),
        out_shape=jax.ShapeDtypeStruct((128, 8, LIVE), BF16),
        compiler_params=params(BIG),
        cost_estimate=cost(0, 1 << 20),
    )(teacher_hidden, student_hidden, token_weight.reshape(1, OWN))


def assemble_call(places, parts, after):
    def kernel(at_ref, *refs):
        out_ref = refs[-1]
        for k in range(4):
            out_ref[pl.ds(pl.multiple_of(256 * at_ref[k], 256), 256), :] = refs[k][:256, :]
            out_ref[pl.ds(pl.multiple_of(1024 + 128 * at_ref[k], 128), 128), :] = refs[k][256:, :]

    return pl.pallas_call(
        kernel,
        in_specs=[SMEM] + [VMEM] * 4 + [ANY] * len(after),
        out_specs=VMEM,
        out_shape=jax.ShapeDtypeStruct((1536, LIVE), BF16),
        compiler_params=params(8),
        cost_estimate=cost(0, 2 << 20),
    )(places, *parts, *after)


def hold_call(values, after):
    n = len(values)

    def kernel(*refs):
        pass

    return pl.pallas_call(
        kernel,
        in_specs=[ANY] * (n + len(after)),
        out_specs=[ANY] * n,
        out_shape=[jax.ShapeDtypeStruct(v.shape, v.dtype) for v in values],
        input_output_aliases={k: k for k in range(n)},
        compiler_params=params(50),
        cost_estimate=cost(0, 0),
    )(*values, *after)


def logits_call(groups, stacks, teacher_head, student_head, prior, last):
    n = len(stacks)

    def kernel(at_ref, ht_ref, hs_ref, *refs):
        refs, (ht_buf, hs_buf, x_buf, sem) = refs[:-4], refs[-4:]
        x_refs, refs = refs[:n], refs[n:]
        if prior is not None:
            old_t, old_s, *refs = refs
        acc_t, acc_s = refs[:2]
        fetch_t, fetch_s = [], []
        for k in range(n):
            g = at_ref[k]
            cols_t = [pl.ds(pl.multiple_of(1024 * g + 512 * j, 512), 512) for j in range(2)]
            cols_s = pl.ds(pl.multiple_of(512 * g, 512), 512)
            x = x_refs[k]
            fetch_t.append(
                [
                    pltpu.make_async_copy(x.at[pl.ds(0, 512), :], x_buf.at[k, pl.ds(0, 512), :], sem.at[k, 0]),
                    pltpu.make_async_copy(ht_ref.at[:, cols_t[0]], ht_buf.at[k, :, pl.ds(0, 512)], sem.at[k, 1]),
                    pltpu.make_async_copy(x.at[pl.ds(512, 512), :], x_buf.at[k, pl.ds(512, 512), :], sem.at[k, 2]),
                    pltpu.make_async_copy(ht_ref.at[:, cols_t[1]], ht_buf.at[k, :, pl.ds(512, 512)], sem.at[k, 5]),
                ]
            )
            fetch_s.append(
                [
                    pltpu.make_async_copy(x.at[pl.ds(1024, 512), :], x_buf.at[k, pl.ds(1024, 512), :], sem.at[k, 3]),
                    pltpu.make_async_copy(hs_ref.at[:, cols_s], hs_buf.at[k], sem.at[k, 4]),
                ]
            )
            for c in fetch_t[k] + fetch_s[k]:
                c.start()
        for k in range(n):
            for c in fetch_t[k][:2]:
                c.wait()
            if k == 0:
                add_t = jnp.dot(ht_buf[0, :, :512], x_buf[0, :512, :], preferred_element_type=F32)
                acc_t[...] = add_t if prior is None else old_t[...] + add_t
            for c in fetch_t[k][2:]:
                c.wait()
            if k == 0:
                acc_t[...] += jnp.dot(ht_buf[0, :, 512:], x_buf[0, 512:1024, :], preferred_element_type=F32)
            else:
                add_t = jnp.dot(ht_buf[k], x_buf[k, :1024, :], preferred_element_type=F32)
            if k > 0:
                acc_t[...] += add_t
            for c in fetch_s[k]:
                c.wait()
            add_s = jnp.dot(hs_buf[k], x_buf[k, 1024:, :], preferred_element_type=F32)
            if k > 0:
                acc_s[...] += add_s
            elif prior is None:
                acc_s[...] = add_s
            else:
                acc_s[...] = old_s[...] + add_s
        if not last:
            refs[2][...] = jnp.zeros((8, 128), F32)
        if last:
            stat_ref, sent_ref = refs[2:]
            t = acc_t[...]
            top_t = jnp.max(t, axis=0, keepdims=True)
            exp_t = jnp.exp(t - top_t)
            sum_t = jnp.sum(exp_t, axis=0, keepdims=True)
            s = acc_s[...]
            cross = jnp.sum(exp_t * (t - s), axis=0, keepdims=True)
            top_s = jnp.max(s, axis=0, keepdims=True)
            sum_s = jnp.sum(jnp.exp(s - top_s), axis=0, keepdims=True)
            lse_t = top_t + jnp.log(sum_t)
            lse_s = top_s + jnp.log(sum_s)
            mean = cross / sum_t
            for j in range(3):
                cols = slice(128 * j, 128 * (j + 1))
                stat_ref[j : j + 1, :] = lse_t[:, cols]
                stat_ref[3 + j : 4 + j, :] = lse_s[:, cols]
                stat_ref[8 + j : 9 + j, :] = mean[:, cols]
            sent_ref[...] = jnp.broadcast_to(stat_ref[:6, :][None], (128, 6, 128))

    args = [groups, teacher_head, student_head, *stacks]
    if prior is not None:
        args += list(prior)
    out_shape = [jax.ShapeDtypeStruct((VOC, LIVE), F32)] * 2
    if last:
        out_shape.append(jax.ShapeDtypeStruct((16, 128), F32))
        out_shape.append(jax.ShapeDtypeStruct((128, 6, 128), F32))
    else:
        out_shape.append(jax.ShapeDtypeStruct((8, 128), F32))
    return pl.pallas_call(
        kernel,
        in_specs=[SMEM] + [ANY] * (n + 2) + [VMEM] * (len(args) - 3 - n),
        out_specs=[VMEM] * len(out_shape),
        out_shape=out_shape,
        input_output_aliases={} if prior is None else {3 + n: 0, 4 + n: 1},
        scratch_shapes=[
            pltpu.VMEM((n, VOC, 1024), BF16),
            pltpu.VMEM((n, VOC, 512), BF16),
            pltpu.VMEM((n, 1536, LIVE), BF16),
            pltpu.SemaphoreType.DMA((n, 6)),
        ],
        compiler_params=params(50),
        cost_estimate=cost(n * 2 * 1536 * LIVE * VOC, n * 8 << 20),
    )(*args)


def logit_grad_call(groups, logits_t, logits_s, stat, all_stats, weight, student_head):
    def kernel(at_ref, t_ref, s_ref, stat_ref, all_ref, w_ref, h_ref, out_ref, g_ref, kl_ref):
        every = all_ref[...]
        top = jnp.max(every, axis=0)
        total = top + jnp.log(jnp.sum(jnp.exp(every - top[None]), axis=0))
        log_zt = jnp.concatenate([total[j : j + 1] for j in range(3)], axis=1)
        log_zs = jnp.concatenate([total[3 + j : 4 + j] for j in range(3)], axis=1)
        own_t = jnp.concatenate([stat_ref[j : j + 1, :] for j in range(3)], axis=1)
        mean = jnp.concatenate([stat_ref[8 + j : 9 + j, :] for j in range(3)], axis=1)
        w = w_ref[...]
        g_ref[...] = (w * (jnp.exp(s_ref[...] - log_zs) - jnp.exp(t_ref[...] - log_zt))).astype(BF16)
        share = jnp.sum(w * mean * jnp.exp(own_t - log_zt), axis=1, keepdims=True)
        common = jnp.sum(w * (log_zs - log_zt), axis=1, keepdims=True)
        kl_ref[0:1, :] = jnp.broadcast_to(share, (1, 128))
        kl_ref[1:2, :] = jnp.broadcast_to(common, (1, 128))
        for k in range(4):
            head = h_ref[:, pl.ds(pl.multiple_of(512 * at_ref[k], 512), 512)]
            out_ref[k] = lax.dot_general(head, g_ref[...], TN, preferred_element_type=F32).astype(BF16)

    return pl.pallas_call(
        kernel,
        in_specs=[SMEM] + [VMEM] * 6,
        out_specs=[VMEM] * 3,
        out_shape=[
            jax.ShapeDtypeStruct((4, 512, LIVE), BF16),
            jax.ShapeDtypeStruct((VOC, LIVE), BF16),
            jax.ShapeDtypeStruct((8, 128), F32),
        ],
        compiler_params=params(16),
        cost_estimate=cost(2 * LIVE * VOC * 2048, 8 << 20, VOC * LIVE * 2),
    )(groups, logits_t, logits_s, stat, all_stats, weight, student_head)


def hidden_half_call(groups, grad, student_head):
    def kernel(at_ref, g_ref, h_ref, out_ref):
        for k in range(4):
            head = h_ref[:, pl.ds(pl.multiple_of(512 * at_ref[k], 512), 512)]
            out_ref[k] = lax.dot_general(head, g_ref[...], TN, preferred_element_type=F32)

    return pl.pallas_call(
        kernel,
        in_specs=[SMEM, VMEM, VMEM],
        out_specs=VMEM,
        out_shape=jax.ShapeDtypeStruct((4, 512, LIVE), F32),
        compiler_params=params(16),
        cost_estimate=cost(2 * LIVE * VOC * 2048, 7 << 20),
    )(groups, grad, student_head)


def head_grad_call(groups, stacks, grad):
    n = len(stacks)

    def kernel(at_ref, g_ref, *refs):
        out_ref, done_ref, x_buf, held_ref, in_sem, out_sem = refs[n:]
        fetch = [
            pltpu.make_async_copy(refs[k].at[pl.ds(1024, 512), :], x_buf.at[k % 2], in_sem.at[k % 2])
            for k in range(n)
        ]
        store = [
            pltpu.make_async_copy(
                held_ref.at[k % 2],
                out_ref.at[:, pl.ds(pl.multiple_of(512 * at_ref[k], 512), 512)],
                out_sem.at[k % 2],
            )
            for k in range(n)
        ]
        fetch[0].start()
        for k in range(n):
            if k + 1 < n:
                fetch[k + 1].start()
            fetch[k].wait()
            if k >= 2:
                store[k - 2].wait()
            held_ref[k % 2] = lax.dot_general(
                g_ref[...], x_buf[k % 2], NT, preferred_element_type=F32
            ).astype(BF16)
            store[k].start()
        done_ref[...] = jnp.zeros((8, 128), F32)
        store[n - 2].wait()
        store[n - 1].wait()

    return pl.pallas_call(
        kernel,
        in_specs=[SMEM, VMEM] + [ANY] * n,
        out_specs=[ANY, VMEM],
        out_shape=[jax.ShapeDtypeStruct((VOC, DS), BF16), jax.ShapeDtypeStruct((8, 128), F32)],
        scratch_shapes=[
            pltpu.VMEM((2, 512, LIVE), BF16),
            pltpu.VMEM((2, VOC, 512), BF16),
            pltpu.SemaphoreType.DMA((2,)),
            pltpu.SemaphoreType.DMA((2,)),
        ],
        compiler_params=params(BIG - 4),
        cost_estimate=cost(2 * LIVE * VOC * DS, 10 << 20),
    )(groups, grad, *stacks)


def join_call(full, half):
    def kernel(f_ref, h_ref, o1_ref, o2_ref, o3_ref, own_ref, f_buf, buf, f_sem, sem):
        full = [pltpu.make_async_copy(f_ref.at[k], f_buf.at[k], f_sem.at[k]) for k in range(4)]
        copies = [pltpu.make_async_copy(h_ref.at[k], buf.at[k], sem.at[k]) for k in range(4)]
        for k in (1, 2, 3, 0):
            full[k].start()
            copies[k].start()
        for k, o_ref in ((1, o1_ref), (2, o2_ref), (3, o3_ref), (0, own_ref)):
            full[k].wait()
            copies[k].wait()
            o_ref[...] = (f_buf[k] + buf[k].astype(F32)).astype(o_ref.dtype)

    return pl.pallas_call(
        kernel,
        in_specs=[ANY, ANY],
        out_specs=[VMEM] * 4,
        out_shape=[jax.ShapeDtypeStruct((512, LIVE), BF16)] * 3 + [jax.ShapeDtypeStruct((512, LIVE), F32)],
        scratch_shapes=[
            pltpu.VMEM((4, 512, LIVE), F32),
            pltpu.VMEM((4, 512, LIVE), BF16),
            pltpu.SemaphoreType.DMA((4,)),
            pltpu.SemaphoreType.DMA((4,)),
        ],
        compiler_params=params(16),
        cost_estimate=cost(0, 8 << 20),
    )(full, half)


def sum_major_call(at, own, came, after):
    def kernel(at_ref, own_ref, c0, c1, c2, after_ref, *refs):
        outs, (buf, sem) = refs[:4], refs[4:]
        copies = [pltpu.make_async_copy(c, buf.at[k], sem.at[k]) for k, c in enumerate((c0, c1, c2))]
        for c in copies:
            c.start()
        for c in copies:
            c.wait()
        for l in (1, 2, 3, 0):
            rows = pl.ds(pl.multiple_of(128 * at_ref[l], 128), 128)
            total = own_ref[rows, :]
            for k in range(3):
                total += buf[k, rows, :].astype(F32)
            outs[l][...] = total.astype(outs[l].dtype)

    return pl.pallas_call(
        kernel,
        in_specs=[SMEM, VMEM, ANY, ANY, ANY, ANY],
        out_specs=[VMEM] * 4,
        out_shape=[jax.ShapeDtypeStruct((128, LIVE), F32)] + [jax.ShapeDtypeStruct((128, LIVE), BF16)] * 3,
        scratch_shapes=[pltpu.VMEM((3, 512, LIVE), BF16), pltpu.SemaphoreType.DMA((3,))],
        compiler_params=params(16),
        cost_estimate=cost(0, 4 << 20),
    )(at, own, *came, after)


def return_call(slot, own, came, kl):
    def kernel(slot_ref, own_ref, c0, c1, c2, kl_ref, out_ref, buf, sem):
        copies = [pltpu.make_async_copy(c, buf.at[k], sem.at[k]) for k, c in enumerate((c0, c1, c2))]
        for c in copies:
            c.start()
        share = kl_ref[0:1, :]
        hi = share.astype(BF16).astype(F32)
        mid = (share - hi).astype(BF16).astype(F32)
        low = share - hi - mid
        lane = lax.broadcasted_iota(jnp.int32, (1, 128), 1)
        extra = jnp.where(lane == 0, hi, jnp.where(lane == 1, mid, jnp.where(lane == 2, low, 0.0)))
        extra = jnp.broadcast_to(extra, (256, 128))
        row = lax.broadcasted_iota(jnp.int32, (256, LIVE), 0)
        eighth = lax.broadcasted_iota(jnp.int32, (256, 128), 0) % 8 == 7
        total = own_ref[...]
        for k in range(3):
            copies[k].wait()
            total += buf[k].astype(F32)
        total = total.astype(BF16)
        for j in range(4):
            pick = jnp.where(row + 256 * j == slot_ref[...], 1.0, 0.0).astype(BF16)
            back = lax.dot_general(pick, total, NT, preferred_element_type=F32)
            back = jnp.where(eighth, extra, back)
            out_ref[32 * j : 32 * (j + 1)] = back.reshape(32, 8, 128).astype(BF16)

    return pl.pallas_call(
        kernel,
        in_specs=[VMEM, VMEM, ANY, ANY, ANY, VMEM],
        out_specs=VMEM,
        out_shape=jax.ShapeDtypeStruct((128, 8, 128), BF16),
        scratch_shapes=[pltpu.VMEM((3, 128, LIVE), BF16), pltpu.SemaphoreType.DMA((3,))],
        compiler_params=params(16),
        cost_estimate=cost(2 * 1024 * LIVE * 128, 2 << 20),
    )(slot, own, *came, kl)


def collect_call(back, kl):
    def kernel(b_ref, kl_ref, out_ref, mean_ref):
        shares = jnp.zeros((8, 128), F32)
        for y in range(4):
            for c in range(2):
                for x in range(4):
                    u = unit_of(y, c, x)
                    total = sum(b_ref[flat(y, c, x, z)].astype(F32) for z in range(4))
                    shares += total
                    out_ref[:, 128 * u : 128 * (u + 1)] = total.astype(BF16)[:OWN]
        row = lax.broadcasted_iota(jnp.int32, (8, 128), 0)
        lane = lax.broadcasted_iota(jnp.int32, (8, 128), 1)
        shares = jnp.where((row == 7) & (lane < 3), shares, 0.0)
        mean_ref[0, 0] = (jnp.sum(shares) + kl_ref[1, 0]) / LIVE

    return pl.pallas_call(
        kernel,
        in_specs=[VMEM, SMEM],
        out_specs=[VMEM, SMEM],
        out_shape=[jax.ShapeDtypeStruct((OWN, DS), BF16), jax.ShapeDtypeStruct((1, 1), F32)],
        compiler_params=params(8),
        cost_estimate=cost(0, 1 << 20),
    )(back, kl)


def local(student_hidden, teacher_hidden, student_head, teacher_head, token_weight, block_count):
    me = lax.axis_index("dp") * 16 + lax.axis_index("vocab")
    y, core, x, z = me // 32, (me // 16) % 2, (me // 4) % 4, me % 4
    turn = jnp.arange(4, dtype=jnp.int32)
    major_at = jnp.where(core == 0, y, x)
    minor_at = jnp.where(core == 0, x, y)

    arrived = lax.all_to_all(
        spread_call(teacher_hidden, student_hidden, token_weight), AXES, split_axis=0, concat_axis=0, tiled=True
    )

    ends = jnp.cumsum(block_count)
    block = jnp.arange(LIVE, dtype=jnp.int32) // BLOCK
    shard = jnp.sum((block[:, None] >= ends[None, :]).astype(jnp.int32), axis=1)
    begin = jnp.sum(jnp.where(jnp.arange(8)[None, :] < shard[:, None], block_count[None, :], 0), axis=1)
    place = (block - begin) * BLOCK + jnp.arange(LIVE, dtype=jnp.int32) % BLOCK
    slot = (shard * 16 + place // OWN) * 8 + place % OWN
    slots = jnp.arange(1024, dtype=jnp.int32)
    pick = (slot[:, None] == slots[None, :]).astype(BF16)
    own = lax.dot_general(
        arrived.reshape(1024, LIVE), pick, (((0,), (1,)), ((), ())), preferred_element_type=F32
    ).astype(BF16)
    weight = lax.dot_general(arrived[:, 7, :8].reshape(1, 1024), pick, NT, preferred_element_type=F32)

    piece = permute(own, across())
    parts = [own] + [permute(own, minor(l)) for l in (1, 2, 3)]
    heads = (teacher_head, student_head)
    stack = assemble_call((minor_at - turn + 4) % 4, parts, (piece,))
    before, after = permute(stack, major(1)), permute(stack, major(3))
    sib_stack = permute(stack, SWAP)
    pieces = [piece] + [permute(piece, along_z(l)) for l in (1, 2, 3)]

    def groups(*steps):
        steps = jnp.array(steps, jnp.int32)
        mine = core * 4 + (major_at - steps + 4) % 4
        theirs = (1 - core) * 4 + (minor_at - steps + 4) % 4
        return mine, theirs

    mine, theirs = groups(0)
    *sums, token = logits_call(jnp.concatenate([mine, theirs]), [stack, sib_stack], *heads, None, False)
    opposite = assemble_call((minor_at + z - turn + 4) % 4, pieces, [token])
    before, after = hold_call([before, after], [token])
    sib_before, sib_after, sib_opposite = (permute(s, SWAP) for s in (before, after, opposite))
    mine, theirs = groups(1, 3)
    *sums, _ = logits_call(mine, [before, after], *heads, sums, False)
    logits_t, logits_s, stat, sent = logits_call(
        jnp.concatenate([theirs, *groups(2)]), [sib_before, sib_after, opposite, sib_opposite], *heads, sums, True
    )
    all_stats = lax.all_to_all(sent, AXES, split_axis=0, concat_axis=0, tiled=True)

    half, grad, kl = logit_grad_call(
        (1 - core) * 4 + (minor_at + turn) % 4, logits_t, logits_s, stat, all_stats, weight, heads[1]
    )
    half = permute(half, SWAP)
    full = hidden_half_call(core * 4 + (major_at + turn) % 4, grad, heads[1])
    mine, theirs = groups(0, 1, 2, 3)
    head_grad, done = head_grad_call(
        jnp.concatenate([mine, theirs]),
        [stack, before, opposite, after, sib_stack, sib_before, sib_opposite, sib_after],
        grad,
    )

    *leave, kept = join_call(full, half)
    came = [permute(leave[k - 1], major(k)) for k in (1, 2, 3)]
    kept, *leave = sum_major_call((minor_at + turn) % 4, kept, came, done)
    came = [permute(leave[l - 1], minor(l)) for l in (1, 2, 3)]
    back = return_call(slot.reshape(1, LIVE), kept, came, kl)
    back = lax.all_to_all(back, AXES, split_axis=0, concat_axis=0, tiled=True)
    hidden_grad, kl_mean = collect_call(back, kl)
    return kl_mean.reshape(()), hidden_grad, head_grad


def solution(mesh):
    rows = P(AXES, None)
    return jax.shard_map(
        local,
        mesh=mesh,
        in_specs=(rows, rows, rows, rows, P(AXES), P()),
        out_specs=(P(), rows, rows),
        check_vma=False,
    )
```
